32 devices in a mesh: tile: 16 (over z, x, core), grp: 2 (over y).
Axes of the slice: x: 2, y: 2, z: 4, core: 2. Of those that a mesh axis runs over, the one named last changes fastest.
Arguments:
- snapshots: float32 [64, 2, 5, 8192], P(None, 'grp', None, 'tile'), may hold values from -2000 to 2000, as said below
- neighbors: int32 [8, 8192], P(None, 'tile'), may hold values from 0 to 767, as said below
- weights: float32 [8, 8192], P(None, 'tile'), may hold values from 0.02 to 0.14
- coupling: float32 [2, 2], replicated, may hold values from -4 to 4
Outputs:
- basis: float32 [64, 2, 5, 8192], P(None, 'grp', None, 'tile')
- coupled: float32 [64, 2, 5, 8192], P(None, 'grp', None, 'tile')
The draws below stay inside these ranges and needn't reach their ends.
Inputs may be any that keep to these rules, and one draw needn't show every extreme that they name: `snapshots`: snapshot values of any sign. `neighbors`: each entry lies within 128 cells of its own cell in the extended block; entry 0 of every cell is the cell 128 before it and entry 1 the cell 128 after it.
All inputs are finite; a program needn't handle non-finite values.
Results may differ from the reference program's by a relative error of at most 0.0055.
Values may be sent and summed in bfloat16 or wider, within the bound.
A program may use at most 64 MiB of HBM per device.

```python
import jax
import jax.numpy as jnp
from jax import lax

SNAPS = 64
FIELDS = 5
NB = 8
HALO = 128
CELLS = 512
CELLS_ALL = 8192
INSTANCES = 2
ROWS_ALL = 81920


def draw_snapshots(key, part):
    key = jax.random.fold_in(key, 11)
    keys = jax.random.split(key, 8)
    shape = (SNAPS, INSTANCES, FIELDS, CELLS_ALL)
    position = jnp.arange(CELLS_ALL, dtype=jnp.float32) / CELLS_ALL
    rough = jnp.exp(jnp.log(2.0) * jax.random.uniform(keys[2], (CELLS_ALL,), jnp.float32))
    trend = jnp.exp(jnp.log(3.0) * position)
    inst_scale = jnp.exp(jax.random.uniform(keys[4], (SNAPS, INSTANCES, 1, 1), jnp.float32, -1.2, 1.2))
    wave = jax.random.randint(keys[5], (SNAPS, INSTANCES, FIELDS, 1), 1, 65).astype(jnp.float32)
    phase = jax.random.uniform(keys[6], (SNAPS, INSTANCES, FIELDS, 1), jnp.float32, 0.0, 6.2831855)
    amplitude = 0.7071 * jnp.exp(jnp.log(5.0) * jax.random.uniform(keys[7], (SNAPS, 1, 1, 1), jnp.float32))
    smooth = amplitude * jnp.sin(6.2831855 * wave * position + phase)
    base = jax.random.truncated_normal(keys[0], -4.0, 4.0, shape, jnp.float32)
    snap_scale = jnp.exp(jnp.log(10.0) * jax.random.uniform(keys[1], (SNAPS, 1, 1, 1), jnp.float32))
    return (base * rough + smooth) * snap_scale * inst_scale * trend


def draw_neighbors(key, part):
    local_cell = jnp.arange(CELLS_ALL, dtype=jnp.int32) % CELLS
    offset = jax.random.randint(key, (NB, CELLS_ALL), 0, 2 * HALO + 1, dtype=jnp.int32)
    offset = offset.at[0].set(0).at[1].set(2 * HALO)
    return (local_cell[None, :] + offset).astype(jnp.int32)


def level_of(key, extent, cuts, smallest, largest):
    def one(axis_at, blocks):
        heights = jax.random.uniform(jax.random.fold_in(jax.random.fold_in(key, 6), axis_at), (blocks,), jnp.float32, smallest / len(cuts), largest / len(cuts))
        return jnp.repeat(jnp.exp(heights), extent[axis_at] // blocks).reshape((-1,) + (1,) * (len(extent) - axis_at - 1))

    factor_of = one(*cuts[0])
    for cut in cuts[1:]:
        factor_of = factor_of * one(*cut)
    return factor_of


def noise(rng, extent, scale, bound, kind=jnp.bfloat16):
    entries = scale * jax.random.normal(rng, extent, jnp.float32)
    return jnp.clip(entries, min=-bound, max=bound).astype(kind)


def setup_inputs(seed: int = 0) -> dict:
    arg_keys = jax.random.split(jax.random.key(seed), 5)
    snapshots = draw_snapshots(jax.random.fold_in(arg_keys[4], 71), 0)
    neighbors = draw_neighbors(jax.random.fold_in(arg_keys[4], 71), 0)
    weights = jnp.clip(0.02 + 0.12000000104308128 * jax.random.uniform(arg_keys[2], (NB, CELLS_ALL), jnp.float32) ** level_of(arg_keys[2], (NB, CELLS_ALL), ((1, 16),), -0.2, 0.2), 0.02, 0.14)
    coupling = noise(arg_keys[3], (INSTANCES, INSTANCES), INSTANCES ** -0.5, 4.0, jnp.float32)
    return dict(snapshots=snapshots, neighbors=neighbors, weights=weights, coupling=coupling)


def reference(snapshots, neighbors, weights, coupling):
    extended = jnp.concatenate([snapshots[..., -HALO:], snapshots, snapshots[..., :HALO]], axis=3)
    offsets = jnp.arange(CELLS_ALL, dtype=jnp.int32) // CELLS * CELLS
    residual = snapshots
    for slot in range(NB):
        picked = jnp.take(extended, (neighbors[slot] + offsets).astype(jnp.int32), axis=3)
        residual = residual - weights[slot] * picked
    flat_rows = residual.reshape(SNAPS, -1)
    gram = jnp.dot(flat_rows, flat_rows.T, precision=lax.Precision.HIGHEST) / ROWS_ALL
    lower = jnp.linalg.cholesky(gram)
    inverse = jax.scipy.linalg.solve_triangular(lower, jnp.eye(SNAPS, dtype=jnp.float32), lower=True)
    basis = jnp.dot(inverse, flat_rows, precision=lax.Precision.HIGHEST).reshape(residual.shape)
    rounded = basis.astype(jnp.bfloat16).astype(jnp.float32)
    mixed = jnp.einsum('nm,kmfc->knfc', coupling, rounded, precision=lax.Precision.HIGHEST)
    return (basis, rounded + mixed)
```

```python
import functools

import jax
import jax.numpy as jnp
from jax import lax
from jax.experimental import pallas as pl
from jax.experimental.pallas import tpu as pltpu
from jax.sharding import PartitionSpec as P

HALO = 128
LANES = 128
MESH = pl.DeviceIdType.MESH
F32 = jnp.float32
BF16 = jnp.bfloat16


def split(value):
    high = value.astype(BF16)
    return high, (value - high.astype(F32)).astype(BF16)


def inverse_factor(gram):
    n = gram.shape[0]
    rows = lax.broadcasted_iota(jnp.int32, (n, n), 0)
    cols = lax.broadcasted_iota(jnp.int32, (n, n), 1)
    both = jnp.concatenate([gram, jnp.where(rows == cols, 1.0, 0.0).astype(F32)], axis=1)
    blocks = [both[8 * b:8 * b + 8] for b in range(n // 8)]
    sub = lax.broadcasted_iota(jnp.int32, (8, 2 * n), 0)
    lane = lax.broadcasted_iota(jnp.int32, (8, 2 * n), 1)
    for j in range(n):
        b, r = divmod(j, 8)
        row = jnp.broadcast_to(blocks[b][r:r + 1], (8, 2 * n))
        inv = 1.0 / jnp.broadcast_to(row[:, j:j + 1], (8, 2 * n))
        scaled = row * inv
        for bb in range(b, n // 8):
            factor = jnp.broadcast_to(blocks[bb][:, j:j + 1], (8, 2 * n))
            if bb == b:
                factor = jnp.where(sub > r, factor, 0.0)
            blocks[bb] = blocks[bb] - factor * scaled
    out = []
    for b in range(n // 8):
        pivot = jnp.sum(jnp.where(lane == sub + 8 * b, blocks[b], 0.0), axis=1, keepdims=True)
        out.append(blocks[b] * lax.rsqrt(pivot))
    return jnp.concatenate(out, axis=0)[:, n:]


def reduce_kernel(dims, x_ref, nbr_ref, w_ref, res_ref, other_ref, inv_ref,
                  edge, halo, stencil, resbf, gsend, grecv, tsend, trecv,
                  hs, hr, s1, r1, s2, r2, s3, r3):
    tiles, grps, low, snaps, fields, chunks = dims
    n1, n2 = low * grps, tiles // low
    me_t, me_g = lax.axis_index("tile"), lax.axis_index("grp")
    right, left = lax.rem(me_t + 1, tiles), lax.rem(me_t + tiles - 1, tiles)
    base, me_low = (me_t // low) * low, lax.rem(me_t, low)
    me1, me2 = me_low * grps + me_g, me_t // low

    def near(d):
        to = lax.rem(me1 + d, n1)
        return (base + to // grps, lax.rem(to, grps))

    def far(d):
        return (lax.rem(me2 + d, n2) * low + me_low, me_g)

    barrier = pltpu.get_barrier_semaphore()
    partners = [(left, me_g), (right, me_g)] + [near(d) for d in range(1, n1)] + [far(d) for d in range(1, n2)]
    for partner in partners:
        pl.semaphore_signal(barrier, inc=1, device_id=partner, device_id_type=MESH)

    step = fields * chunks

    def chunk(q):
        return jnp.concatenate(
            [x_ref[pl.ds(f * chunks + q, snaps, stride=step), :] for f in range(fields)], axis=0)

    edge[0] = chunk(chunks - 1).astype(BF16)
    edge[1] = chunk(0).astype(BF16)
    pl.semaphore_wait(barrier, len(partners))
    sends = []
    for side, to in ((0, right), (1, left)):
        copy = pltpu.make_async_remote_copy(
            src_ref=edge.at[side], dst_ref=halo.at[side], send_sem=hs.at[side], recv_sem=hr.at[side],
            device_id=(to, me_g), device_id_type=MESH)
        copy.start()
        sends.append(copy)

    iota = lax.broadcasted_iota(jnp.int32, (3 * LANES, LANES), 0)
    for q in range(chunks):
        here = slice(q * LANES, (q + 1) * LANES)
        total = jnp.zeros((3 * LANES, LANES), F32)
        for j in range(nbr_ref.shape[0]):
            total = total + jnp.where(iota == nbr_ref[j:j + 1, here] - q * LANES, w_ref[j:j + 1, here], 0.0)
        stencil[q] = total.astype(BF16)

    own = [chunk(q).astype(BF16) for q in range(chunks)]

    def part(q, d, block):
        return jnp.dot(block, stencil[q, d * LANES:(d + 1) * LANES, :], preferred_element_type=F32)

    sums = []
    for q in range(chunks):
        total = None
        for d in range(3):
            if 0 <= q + d - 1 < chunks:
                term = part(q, d, own[q + d - 1])
                total = term if total is None else total + term
        sums.append(total)
    for copy in sends:
        copy.wait()
    sums[0] = sums[0] + part(0, 0, halo[0])
    sums[-1] = sums[-1] + part(chunks - 1, 2, halo[1])
    highs, lows = [], []
    rows = snaps * fields
    for q in range(chunks):
        res = chunk(q) - sums[q]
        res_ref[q * rows:(q + 1) * rows, :] = res
        high, low_part = split(res)
        resbf[q * rows:(q + 1) * rows, :] = high
        highs.append(high)
        lows.append(low_part)

    gram = jnp.zeros((2 * snaps, snaps), F32)
    for f in range(fields):
        at = slice(f * snaps, (f + 1) * snaps)
        high = jnp.concatenate([h[at] for h in highs], axis=1)
        low_part = jnp.concatenate([h[at] for h in lows], axis=1)
        gram = gram + lax.dot_general(jnp.concatenate([high, low_part], axis=0), high,
                                      (((1,), (1,)), ((), ())), preferred_element_type=F32)
    gram = gram[:snaps] + (gram[snaps:] + gram[snaps:].T)
    gram = gram * (1.0 / (fields * chunks * LANES * tiles * grps))
    half = snaps // 2
    gsend[...] = jnp.concatenate([gram[:half], gram[half:]], axis=1)

    def exchange(count, where, src, dst, ss, rs):
        copies = []
        for d in range(1, count):
            copy = pltpu.make_async_remote_copy(
                src_ref=src, dst_ref=dst.at[d - 1], send_sem=ss.at[d - 1], recv_sem=rs.at[d - 1],
                device_id=where(d), device_id_type=MESH)
            copy.start()
            copies.append(copy)
        return copies

    copies = exchange(n1, near, gsend, grecv, s1, r1)
    total = gsend[...]
    for d, copy in enumerate(copies):
        copy.wait_recv()
        total = total + grecv[d]
    tsend[...] = total
    far_copies = exchange(n2, far, tsend, trecv, s2, r2)
    res_copies = exchange(grps, lambda d: (me_t, lax.rem(me_g + d, grps)), resbf, other_ref, s3, r3)
    for d, copy in enumerate(far_copies):
        copy.wait_recv()
        total = total + trecv[d]
    gram = jnp.concatenate([total[:, :snaps], total[:, snaps:]], axis=0)
    inv_ref[...] = inverse_factor(gram)
    for copy in copies + far_copies:
        copy.wait_send()
    for copy in res_copies:
        copy.wait()


def basis_kernel(dims, inv_ref, res_ref, other_ref, coupling_ref, basis_ref, coupled_ref):
    tiles, grps, low, snaps, fields, chunks = dims
    me_g = lax.axis_index("grp")
    rows, step = snaps * fields, fields * chunks
    high, low_part = split(inv_ref[...])
    three = jnp.concatenate([high, low_part, high], axis=1)
    two = jnp.concatenate([high, low_part], axis=1)
    own_scale = coupling_ref[me_g, me_g]
    scales = [coupling_ref[me_g, lax.rem(me_g + grps - d, grps)] for d in range(1, grps)]
    for f in range(fields):
        for q in range(chunks):
            at = pl.ds(q * rows + f * snaps, snaps)
            to = pl.ds(f * chunks + q, snaps, stride=step)
            rh, rl = split(res_ref[at, :])
            basis = jnp.dot(three, jnp.concatenate([rh, rh, rl], axis=0), preferred_element_type=F32)
            basis_ref[to, :] = basis
            rounded = basis.astype(BF16).astype(F32)
            mixed = own_scale * rounded
            for d in range(1, grps):
                there = other_ref[d - 1, at, :]
                theirs = jnp.dot(two, jnp.concatenate([there, there], axis=0), preferred_element_type=F32)
                mixed = mixed + scales[d - 1] * theirs.astype(BF16).astype(F32)
            coupled_ref[to, :] = rounded + mixed


def local(mesh, snapshots, neighbors, weights, coupling):
    tiles, grps = mesh.shape["tile"], mesh.shape["grp"]
    snaps, _, fields, cells = snapshots.shape
    chunks = cells // LANES
    low = 4
    dims = (tiles, grps, low, snaps, fields, chunks)
    n1, n2 = low * grps, tiles // low
    rows = snaps * fields
    count = rows * chunks
    x = snapshots.reshape(count, LANES)
    vmem = pl.BlockSpec(memory_space=pltpu.VMEM)
    dma = lambda n: pltpu.SemaphoreType.DMA((n,))
    res, other, inverse = pl.pallas_call(
        functools.partial(reduce_kernel, dims),
        out_shape=(jax.ShapeDtypeStruct((count, LANES), F32),
                   jax.ShapeDtypeStruct((grps - 1, count, LANES), BF16),
                   jax.ShapeDtypeStruct((snaps, snaps), F32)),
        in_specs=[vmem] * 3,
        out_specs=(vmem,) * 3,
        scratch_shapes=[
            pltpu.VMEM((2, rows, LANES), BF16),
            pltpu.VMEM((2, rows, LANES), BF16),
            pltpu.VMEM((chunks, 3 * LANES, LANES), BF16),
            pltpu.VMEM((count, LANES), BF16),
            pltpu.VMEM((snaps // 2, 2 * snaps), F32),
            pltpu.VMEM((n1 - 1, snaps // 2, 2 * snaps), F32),
            pltpu.VMEM((snaps // 2, 2 * snaps), F32),
            pltpu.VMEM((n2 - 1, snaps // 2, 2 * snaps), F32),
            dma(2), dma(2), dma(n1 - 1), dma(n1 - 1), dma(n2 - 1), dma(n2 - 1), dma(grps - 1), dma(grps - 1),
        ],
        compiler_params=pltpu.CompilerParams(
            collective_id=0, has_side_effects=True, vmem_limit_bytes=32 * 2 ** 20),
        name="reduce",
    )(x, neighbors, weights)
    basis, coupled = pl.pallas_call(
        functools.partial(basis_kernel, dims),
        out_shape=(jax.ShapeDtypeStruct((count, LANES), F32),) * 2,
        in_specs=[vmem] * 3 + [pl.BlockSpec(memory_space=pltpu.SMEM)],
        out_specs=(vmem,) * 2,
        compiler_params=pltpu.CompilerParams(vmem_limit_bytes=32 * 2 ** 20),
        name="basis",
    )(inverse, res, other, coupling)
    return basis.reshape(snapshots.shape), coupled.reshape(snapshots.shape)


def solution(mesh):
    return jax.shard_map(
        functools.partial(local, mesh),
        mesh=mesh,
        in_specs=(P(None, "grp", None, "tile"), P(None, "tile"), P(None, "tile"), P()),
        out_specs=(P(None, "grp", None, "tile"), P(None, "grp", None, "tile")),
        check_vma=False,
    )
```

```python
import functools

import jax
import jax.numpy as jnp
from jax import lax
from jax.experimental import pallas as pl
from jax.experimental.pallas import tpu as pltpu
from jax.sharding import PartitionSpec as P

HALO = 128
LANES = 128
MESH = pl.DeviceIdType.MESH
F32 = jnp.float32
BF16 = jnp.bfloat16


def split(value):
    high = value.astype(BF16)
    return high, (value - high.astype(F32)).astype(BF16)


def inverse_factor(gram):
    n, p = gram.shape[0], 8
    w = 2 * n
    rows = lax.broadcasted_iota(jnp.int32, (n, n), 0)
    cols = lax.broadcasted_iota(jnp.int32, (n, n), 1)
    both = jnp.concatenate([gram, jnp.where(rows == cols, 1.0, 0.0).astype(F32)], axis=1)
    blocks = [both[p * b:p * b + p] for b in range(n // p)]
    sub = lax.broadcasted_iota(jnp.int32, (p, w), 0)

    def full(value):
        return jnp.broadcast_to(value, (p, w))

    out = []
    for b in range(n // p):
        c = p * b
        row = [full(blocks[b][r:r + 1]) for r in range(p)]
        a = {(r, s): full(row[r][:, c + s:c + s + 1]) for r in range(p) for s in range(r, p)}
        inv = []
        for r in range(p):
            inv.append(1.0 / a[r, r])
            for s in range(r + 1, p):
                m = a[r, s] * inv[r]
                row[s] = row[s] - m * row[r]
                for t in range(s, p):
                    a[s, t] = a[s, t] - m * a[r, t]
        for bb in range(b + 1, n // p):
            col = [full(blocks[bb][:, c + s:c + s + 1]) for s in range(p)]
            for r in range(p):
                factor = col[r] * inv[r]
                for s in range(r + 1, p):
                    col[s] = col[s] - factor * a[r, s]
                blocks[bb] = blocks[bb] - factor * row[r]
        done, pivot = row[0], a[0, 0]
        for r in range(1, p):
            done = jnp.where(sub == r, row[r], done)
            pivot = jnp.where(sub == r, a[r, r], pivot)
        out.append(done * lax.rsqrt(pivot))
    return jnp.concatenate(out, axis=0)[:, n:]


def reduce_kernel(dims, x_hbm, nbr_hbm, w_hbm, coupling_hbm, res_ref, other_ref, inv_ref, coupling_ref,
                  x_ref, nbr_ref, w_ref, pairs, edge, halo, stencil, resbf, gsend, grecv, tsend, trecv,
                  hs, hr, s1, r1, s2, r2, s3, r3, loads):
    tiles, grps, low, snaps, fields, chunks = dims
    n1, n2 = low * grps, tiles // low
    me_t, me_g = lax.axis_index("tile"), lax.axis_index("grp")
    right, left = lax.rem(me_t + 1, tiles), lax.rem(me_t + tiles - 1, tiles)
    base, me_low = (me_t // low) * low, lax.rem(me_t, low)
    me1, me2 = me_low * grps + me_g, me_t // low

    def near(d):
        to = lax.rem(me1 + d, n1)
        return (base + to // grps, lax.rem(to, grps))

    def far(d):
        return (lax.rem(me2 + d, n2) * low + me_low, me_g)

    barrier = pltpu.get_barrier_semaphore()
    partners = [(left, me_g), (right, me_g)] + [near(d) for d in range(1, n1)] + [far(d) for d in range(1, n2)]
    for partner in partners:
        pl.semaphore_signal(barrier, inc=1, device_id=partner, device_id_type=MESH)

    ins = [pltpu.make_async_copy(src, dst, loads.at[i]) for i, (src, dst) in enumerate(
        ((x_hbm, x_ref), (nbr_hbm, nbr_ref), (w_hbm, w_ref), (coupling_hbm, pairs)))]
    for copy in (ins[1], ins[2], ins[0], ins[3]):
        copy.start()
    step = fields * chunks

    def chunk(q):
        return jnp.concatenate(
            [x_ref[pl.ds(f * chunks + q, snaps, stride=step), :] for f in range(fields)], axis=0)

    ins[1].wait()
    ins[2].wait()
    iota = lax.broadcasted_iota(jnp.int32, (3 * LANES, LANES), 0)
    for q in range(chunks):
        here = slice(q * LANES, (q + 1) * LANES)
        total = jnp.zeros((3 * LANES, LANES), F32)
        for j in range(nbr_ref.shape[0]):
            total = total + jnp.where(iota == nbr_ref[j:j + 1, here] - q * LANES, w_ref[j:j + 1, here], 0.0)
        stencil[q] = total.astype(BF16)

    ins[0].wait()
    edge[0] = chunk(chunks - 1).astype(BF16)
    edge[1] = chunk(0).astype(BF16)
    pl.semaphore_wait(barrier, len(partners))
    sends = []
    for side, to in ((0, right), (1, left)):
        copy = pltpu.make_async_remote_copy(
            src_ref=edge.at[side], dst_ref=halo.at[side], send_sem=hs.at[side], recv_sem=hr.at[side],
            device_id=(to, me_g), device_id_type=MESH)
        copy.start()
        sends.append(copy)

    own = [chunk(q).astype(BF16) for q in range(chunks)]

    def part(q, d, block):
        return jnp.dot(block, stencil[q, d * LANES:(d + 1) * LANES, :], preferred_element_type=F32)

    sums = []
    for q in range(chunks):
        total = None
        for d in range(3):
            if 0 <= q + d - 1 < chunks:
                term = part(q, d, own[q + d - 1])
                total = term if total is None else total + term
        sums.append(total)
    for copy in sends:
        copy.wait()
    sums[0] = sums[0] + part(0, 0, halo[0])
    sums[-1] = sums[-1] + part(chunks - 1, 2, halo[1])
    highs, lows = [], []
    rows = snaps * fields
    for q in range(chunks):
        res = chunk(q) - sums[q]
        res_ref[q * rows:(q + 1) * rows, :] = res
        high, low_part = split(res)
        resbf[q * rows:(q + 1) * rows, :] = high
        highs.append(high)
        lows.append(low_part)

    gram = jnp.zeros((2 * snaps, snaps), F32)
    for f in range(fields):
        at = slice(f * snaps, (f + 1) * snaps)
        high = jnp.concatenate([h[at] for h in highs], axis=1)
        low_part = jnp.concatenate([h[at] for h in lows], axis=1)
        gram = gram + lax.dot_general(jnp.concatenate([high, low_part], axis=0), high,
                                      (((1,), (1,)), ((), ())), preferred_element_type=F32)
    gram = gram[:snaps] + (gram[snaps:] + gram[snaps:].T)
    gram = gram * (1.0 / (fields * chunks * LANES * tiles * grps))
    half = snaps // 2
    gsend[...] = jnp.concatenate([gram[:half], gram[half:]], axis=1)

    def exchange(count, where, src, dst, ss, rs):
        copies = []
        for d in range(1, count):
            copy = pltpu.make_async_remote_copy(
                src_ref=src, dst_ref=dst.at[d - 1], send_sem=ss.at[d - 1], recv_sem=rs.at[d - 1],
                device_id=where(d), device_id_type=MESH)
            copy.start()
            copies.append(copy)
        return copies

    copies = exchange(n1, near, gsend, grecv, s1, r1)
    total = gsend[...]
    for d, copy in enumerate(copies):
        copy.wait_recv()
        total = total + grecv[d]
    tsend[...] = total
    far_copies = exchange(n2, far, tsend, trecv, s2, r2)
    res_copies = exchange(grps, lambda d: (me_t, lax.rem(me_g + d, grps)), resbf, other_ref, s3, r3)
    for d, copy in enumerate(far_copies):
        copy.wait_recv()
        total = total + trecv[d]
    gram = jnp.concatenate([total[:, :snaps], total[:, snaps:]], axis=0)
    inv_ref[...] = inverse_factor(gram)
    ins[3].wait()
    coupling_ref[...] = pairs[...]
    for copy in copies + far_copies:
        copy.wait_send()
    for copy in res_copies:
        copy.wait()


def basis_kernel(dims, inv_ref, res_ref, other_ref, coupling_ref, basis_ref, coupled_ref):
    tiles, grps, low, snaps, fields, chunks = dims
    me_g = lax.axis_index("grp")
    rows, step = snaps * fields, fields * chunks
    high, low_part = split(inv_ref[...])
    three = jnp.concatenate([high, low_part, high], axis=1)
    two = jnp.concatenate([high, low_part], axis=1)
    rows_at = lax.broadcasted_iota(jnp.int32, (grps, grps), 0)
    cols_at = lax.broadcasted_iota(jnp.int32, (grps, grps), 1)

    def scale(d):
        here = (rows_at == me_g) & (cols_at == lax.rem(me_g + grps - d, grps))
        kept = jnp.where(here, coupling_ref[...], 0.0)
        return jnp.sum(jnp.sum(kept, axis=1, keepdims=True), axis=0, keepdims=True)

    own_scale = scale(0)
    scales = [scale(d) for d in range(1, grps)]
    for f in range(fields):
        for q in range(chunks):
            at = pl.ds(q * rows + f * snaps, snaps)
            to = pl.ds(f * chunks + q, snaps, stride=step)
            rh, rl = split(res_ref[at, :])
            basis = jnp.dot(three, jnp.concatenate([rh, rh, rl], axis=0), preferred_element_type=F32)
            basis_ref[to, :] = basis
            rounded = basis.astype(BF16).astype(F32)
            mixed = own_scale * rounded
            for d in range(1, grps):
                there = other_ref[d - 1, at, :]
                theirs = jnp.dot(two, jnp.concatenate([there, there], axis=0), preferred_element_type=F32)
                mixed = mixed + scales[d - 1] * theirs.astype(BF16).astype(F32)
            coupled_ref[to, :] = rounded + mixed


def local(mesh, snapshots, neighbors, weights, coupling):
    tiles, grps = mesh.shape["tile"], mesh.shape["grp"]
    snaps, _, fields, cells = snapshots.shape
    chunks = cells // LANES
    low = 4
    dims = (tiles, grps, low, snaps, fields, chunks)
    n1, n2 = low * grps, tiles // low
    rows = snaps * fields
    count = rows * chunks
    x = snapshots.reshape(count, LANES)
    vmem = pl.BlockSpec(memory_space=pltpu.VMEM)
    dma = lambda n: pltpu.SemaphoreType.DMA((n,))
    res, other, inverse, pairs = pl.pallas_call(
        functools.partial(reduce_kernel, dims),
        out_shape=(jax.ShapeDtypeStruct((count, LANES), F32),
                   jax.ShapeDtypeStruct((grps - 1, count, LANES), BF16),
                   jax.ShapeDtypeStruct((snaps, snaps), F32),
                   jax.ShapeDtypeStruct(coupling.shape, F32)),
        in_specs=[pl.BlockSpec(memory_space=pltpu.HBM)] * 4,
        out_specs=(vmem,) * 4,
        scratch_shapes=[
            pltpu.VMEM((count, LANES), F32),
            pltpu.VMEM(neighbors.shape, jnp.int32),
            pltpu.VMEM(weights.shape, F32),
            pltpu.VMEM(coupling.shape, F32),
            pltpu.VMEM((2, rows, LANES), BF16),
            pltpu.VMEM((2, rows, LANES), BF16),
            pltpu.VMEM((chunks, 3 * LANES, LANES), BF16),
            pltpu.VMEM((count, LANES), BF16),
            pltpu.VMEM((snaps // 2, 2 * snaps), F32),
            pltpu.VMEM((n1 - 1, snaps // 2, 2 * snaps), F32),
            pltpu.VMEM((snaps // 2, 2 * snaps), F32),
            pltpu.VMEM((n2 - 1, snaps // 2, 2 * snaps), F32),
            dma(2), dma(2), dma(n1 - 1), dma(n1 - 1), dma(n2 - 1), dma(n2 - 1), dma(grps - 1), dma(grps - 1),
            dma(4),
        ],
        compiler_params=pltpu.CompilerParams(
            collective_id=0, has_side_effects=True, vmem_limit_bytes=32 * 2 ** 20),
        name="reduce",
    )(*[pltpu.with_memory_space_constraint(a, pltpu.HBM) for a in (x, neighbors, weights, coupling)])
    basis, coupled = pl.pallas_call(
        functools.partial(basis_kernel, dims),
        out_shape=(jax.ShapeDtypeStruct((count, LANES), F32),) * 2,
        in_specs=[vmem] * 4,
        out_specs=(vmem,) * 2,
        compiler_params=pltpu.CompilerParams(vmem_limit_bytes=32 * 2 ** 20),
        name="basis",
    )(inverse, res, other, pairs)
    return basis.reshape(snapshots.shape), coupled.reshape(snapshots.shape)


def solution(mesh):
    return jax.shard_map(
        functools.partial(local, mesh),
        mesh=mesh,
        in_specs=(P(None, "grp", None, "tile"), P(None, "tile"), P(None, "tile"), P()),
        out_specs=(P(None, "grp", None, "tile"), P(None, "grp", None, "tile")),
        check_vma=False,
    )
```

```python
import functools

import jax
import jax.numpy as jnp
from jax import lax
from jax.experimental import pallas as pl
from jax.experimental.pallas import tpu as pltpu
from jax.sharding import PartitionSpec as P

HALO = 128
LANES = 128
MESH = pl.DeviceIdType.MESH
F32 = jnp.float32
BF16 = jnp.bfloat16


def split(value):
    high = value.astype(BF16)
    return high, (value - high.astype(F32)).astype(BF16)


def inverse_factor(gram):
    n, p = gram.shape[0], 8
    w = 2 * n
    rows = lax.broadcasted_iota(jnp.int32, (n, n), 0)
    cols = lax.broadcasted_iota(jnp.int32, (n, n), 1)
    both = jnp.concatenate([gram, jnp.where(rows == cols, 1.0, 0.0).astype(F32)], axis=1)
    blocks = [both[p * b:p * b + p] for b in range(n // p)]
    sub = lax.broadcasted_iota(jnp.int32, (p, w), 0)

    def full(value):
        return jnp.broadcast_to(value, (p, w))

    out = []
    for b in range(n // p):
        c = p * b
        row = [full(blocks[b][r:r + 1]) for r in range(p)]
        a = {(r, s): full(row[r][:, c + s:c + s + 1]) for r in range(p) for s in range(r, p)}
        inv = []
        for r in range(p):
            inv.append(1.0 / a[r, r])
            for s in range(r + 1, p):
                m = a[r, s] * inv[r]
                row[s] = row[s] - m * row[r]
                for t in range(s, p):
                    a[s, t] = a[s, t] - m * a[r, t]
        for bb in range(b + 1, n // p):
            col = [full(blocks[bb][:, c + s:c + s + 1]) for s in range(p)]
            for r in range(p):
                factor = col[r] * inv[r]
                for s in range(r + 1, p):
                    col[s] = col[s] - factor * a[r, s]
                blocks[bb] = blocks[bb] - factor * row[r]
        done, pivot = row[0], a[0, 0]
        for r in range(1, p):
            done = jnp.where(sub == r, row[r], done)
            pivot = jnp.where(sub == r, a[r, r], pivot)
        out.append(done * lax.rsqrt(pivot))
    return jnp.concatenate(out, axis=0)[:, n:]


def reduce_kernel(dims, x_hbm, nbr_hbm, w_hbm, coupling_hbm, res_ref, other_ref, inv_ref, coupling_ref,
                  x_ref, nbr_ref, w_ref, pairs, edge, halo, stencil, resbf, gsend, grecv, tsend, trecv,
                  hs, hr, s1, r1, s2, r2, s3, r3, loads):
    tiles, grps, low, snaps, fields, chunks = dims
    n1, n2 = low * grps, tiles // low
    me_t, me_g = lax.axis_index("tile"), lax.axis_index("grp")
    right, left = lax.rem(me_t + 1, tiles), lax.rem(me_t + tiles - 1, tiles)
    base, me_low = (me_t // low) * low, lax.rem(me_t, low)
    me1, me2 = me_low * grps + me_g, me_t // low

    def near(d):
        to = lax.rem(me1 + d, n1)
        return (base + to // grps, lax.rem(to, grps))

    def far(d):
        return (lax.rem(me2 + d, n2) * low + me_low, me_g)

    barrier = pltpu.get_barrier_semaphore()
    partners = [(left, me_g), (right, me_g)] + [near(d) for d in range(1, n1)] + [far(d) for d in range(1, n2)]
    for partner in partners:
        pl.semaphore_signal(barrier, inc=1, device_id=partner, device_id_type=MESH)

    ins = [pltpu.make_async_copy(src, dst, loads.at[i]) for i, (src, dst) in enumerate(
        ((x_hbm, x_ref), (nbr_hbm, nbr_ref), (w_hbm, w_ref), (coupling_hbm, pairs)))]
    for copy in (ins[1], ins[2], ins[0], ins[3]):
        copy.start()
    step = fields * chunks

    def chunk(q):
        return jnp.concatenate(
            [x_ref[pl.ds(f * chunks + q, snaps, stride=step), :] for f in range(fields)], axis=0)

    ins[1].wait()
    ins[2].wait()
    iota = lax.broadcasted_iota(jnp.int32, (3 * LANES, LANES), 0)
    for q in range(chunks):
        here = slice(q * LANES, (q + 1) * LANES)
        total = jnp.zeros((3 * LANES, LANES), F32)
        for j in range(nbr_ref.shape[0]):
            total = total + jnp.where(iota == nbr_ref[j:j + 1, here] - q * LANES, w_ref[j:j + 1, here], 0.0)
        stencil[q] = total.astype(BF16)

    ins[0].wait()
    edge[0] = chunk(chunks - 1).astype(BF16)
    edge[1] = chunk(0).astype(BF16)
    pl.semaphore_wait(barrier, len(partners))
    sends = []
    for side, to in ((0, right), (1, left)):
        copy = pltpu.make_async_remote_copy(
            src_ref=edge.at[side], dst_ref=halo.at[side], send_sem=hs.at[side], recv_sem=hr.at[side],
            device_id=(to, me_g), device_id_type=MESH)
        copy.start()
        sends.append(copy)

    own = [chunk(q).astype(BF16) for q in range(chunks)]

    def part(q, d, block):
        return jnp.dot(block, stencil[q, d * LANES:(d + 1) * LANES, :], preferred_element_type=F32)

    rows = snaps * fields
    highs, lows = [None] * chunks, [None] * chunks
    res_copies = []
    early = 1

    def send_res(q):
        for d in range(1, grps):
            at = pl.ds(q * rows, rows)
            copy = pltpu.make_async_remote_copy(
                src_ref=resbf.at[at], dst_ref=other_ref.at[d - 1, at],
                send_sem=s3.at[d - 1, q], recv_sem=r3.at[d - 1, q],
                device_id=(me_t, lax.rem(me_g + d, grps)), device_id_type=MESH)
            copy.start()
            res_copies.append(copy)

    def finish(q, stencil_sum):
        res = chunk(q) - stencil_sum
        res_ref[q * rows:(q + 1) * rows, :] = res
        highs[q], lows[q] = split(res)
        resbf[q * rows:(q + 1) * rows, :] = highs[q]

    sums = []
    for q in range(chunks):
        total = None
        for d in range(3):
            if 0 <= q + d - 1 < chunks:
                term = part(q, d, own[q + d - 1])
                total = term if total is None else total + term
        sums.append(total)
    for q in range(1, chunks - 1):
        finish(q, sums[q])
        if q == early:
            send_res(q)
    for copy in sends:
        copy.wait()
    finish(0, sums[0] + part(0, 0, halo[0]))
    finish(chunks - 1, sums[-1] + part(chunks - 1, 2, halo[1]))

    gram = jnp.zeros((2 * snaps, snaps), F32)
    for f in range(fields):
        at = slice(f * snaps, (f + 1) * snaps)
        high = jnp.concatenate([h[at] for h in highs], axis=1)
        low_part = jnp.concatenate([h[at] for h in lows], axis=1)
        gram = gram + lax.dot_general(jnp.concatenate([high, low_part], axis=0), high,
                                      (((1,), (1,)), ((), ())), preferred_element_type=F32)
    gram = gram[:snaps] + (gram[snaps:] + gram[snaps:].T)
    gram = gram * (1.0 / (fields * chunks * LANES * tiles * grps))
    half = snaps // 2
    gsend[...] = jnp.concatenate([gram[:half], gram[half:]], axis=1)

    def exchange(count, where, src, dst, ss, rs):
        copies = []
        for d in range(1, count):
            copy = pltpu.make_async_remote_copy(
                src_ref=src, dst_ref=dst.at[d - 1], send_sem=ss.at[d - 1], recv_sem=rs.at[d - 1],
                device_id=where(d), device_id_type=MESH)
            copy.start()
            copies.append(copy)
        return copies

    total = gsend[...]
    copies = exchange(n1, near, gsend, grecv, s1, r1)
    for q in range(chunks):
        if q != early:
            send_res(q)
    for d, copy in enumerate(copies):
        copy.wait_recv()
        total = total + grecv[d]
    tsend[...] = total
    far_copies = exchange(n2, far, tsend, trecv, s2, r2)
    for d, copy in enumerate(far_copies):
        copy.wait_recv()
        total = total + trecv[d]
    gram = jnp.concatenate([total[:, :snaps], total[:, snaps:]], axis=0)
    inv_ref[...] = inverse_factor(gram)
    ins[3].wait()
    coupling_ref[...] = pairs[...]
    for copy in copies + far_copies:
        copy.wait_send()
    for copy in res_copies:
        copy.wait()


def basis_kernel(dims, inv_ref, res_ref, other_ref, coupling_ref, basis_ref, coupled_ref):
    tiles, grps, low, snaps, fields, chunks = dims
    me_g = lax.axis_index("grp")
    rows, step = snaps * fields, fields * chunks
    high, low_part = split(inv_ref[...])
    three = jnp.concatenate([high, low_part, high], axis=1)
    two = jnp.concatenate([high, low_part], axis=1)
    rows_at = lax.broadcasted_iota(jnp.int32, (grps, grps), 0)
    cols_at = lax.broadcasted_iota(jnp.int32, (grps, grps), 1)

    def scale(d):
        here = (rows_at == me_g) & (cols_at == lax.rem(me_g + grps - d, grps))
        kept = jnp.where(here, coupling_ref[...], 0.0)
        return jnp.sum(jnp.sum(kept, axis=1, keepdims=True), axis=0, keepdims=True)

    own_scale = scale(0)
    scales = [scale(d) for d in range(1, grps)]
    for f in range(fields):
        for q in range(chunks):
            at = pl.ds(q * rows + f * snaps, snaps)
            to = pl.ds(f * chunks + q, snaps, stride=step)
            rh, rl = split(res_ref[at, :])
            basis = jnp.dot(three, jnp.concatenate([rh, rh, rl], axis=0), preferred_element_type=F32)
            basis_ref[to, :] = basis
            rounded = basis.astype(BF16).astype(F32)
            mixed = own_scale * rounded
            for d in range(1, grps):
                there = other_ref[d - 1, at, :]
                theirs = jnp.dot(two, jnp.concatenate([there, there], axis=0), preferred_element_type=F32)
                mixed = mixed + scales[d - 1] * theirs.astype(BF16).astype(F32)
            coupled_ref[to, :] = rounded + mixed


def local(mesh, snapshots, neighbors, weights, coupling):
    tiles, grps = mesh.shape["tile"], mesh.shape["grp"]
    snaps, _, fields, cells = snapshots.shape
    chunks = cells // LANES
    low = 4
    dims = (tiles, grps, low, snaps, fields, chunks)
    n1, n2 = low * grps, tiles // low
    rows = snaps * fields
    count = rows * chunks
    x = snapshots.reshape(count, LANES)
    vmem = pl.BlockSpec(memory_space=pltpu.VMEM)
    dma = lambda n: pltpu.SemaphoreType.DMA((n,))
    res, other, inverse, pairs = pl.pallas_call(
        functools.partial(reduce_kernel, dims),
        out_shape=(jax.ShapeDtypeStruct((count, LANES), F32),
                   jax.ShapeDtypeStruct((grps - 1, count, LANES), BF16),
                   jax.ShapeDtypeStruct((snaps, snaps), F32),
                   jax.ShapeDtypeStruct(coupling.shape, F32)),
        in_specs=[pl.BlockSpec(memory_space=pltpu.HBM)] * 4,
        out_specs=(vmem,) * 4,
        scratch_shapes=[
            pltpu.VMEM((count, LANES), F32),
            pltpu.VMEM(neighbors.shape, jnp.int32),
            pltpu.VMEM(weights.shape, F32),
            pltpu.VMEM(coupling.shape, F32),
            pltpu.VMEM((2, rows, LANES), BF16),
            pltpu.VMEM((2, rows, LANES), BF16),
            pltpu.VMEM((chunks, 3 * LANES, LANES), BF16),
            pltpu.VMEM((count, LANES), BF16),
            pltpu.VMEM((snaps // 2, 2 * snaps), F32),
            pltpu.VMEM((n1 - 1, snaps // 2, 2 * snaps), F32),
            pltpu.VMEM((snaps // 2, 2 * snaps), F32),
            pltpu.VMEM((n2 - 1, snaps // 2, 2 * snaps), F32),
            dma(2), dma(2), dma(n1 - 1), dma(n1 - 1), dma(n2 - 1), dma(n2 - 1), pltpu.SemaphoreType.DMA((grps - 1, chunks)), pltpu.SemaphoreType.DMA((grps - 1, chunks)),
            dma(4),
        ],
        compiler_params=pltpu.CompilerParams(
            collective_id=0, has_side_effects=True, vmem_limit_bytes=32 * 2 ** 20),
        name="reduce",
    )(*[pltpu.with_memory_space_constraint(a, pltpu.HBM) for a in (x, neighbors, weights, coupling)])
    basis, coupled = pl.pallas_call(
        functools.partial(basis_kernel, dims),
        out_shape=(jax.ShapeDtypeStruct((count, LANES), F32),) * 2,
        in_specs=[vmem] * 4,
        out_specs=(vmem,) * 2,
        compiler_params=pltpu.CompilerParams(vmem_limit_bytes=32 * 2 ** 20),
        name="basis",
    )(inverse, res, other, pairs)
    return basis.reshape(snapshots.shape), coupled.reshape(snapshots.shape)


def solution(mesh):
    return jax.shard_map(
        functools.partial(local, mesh),
        mesh=mesh,
        in_specs=(P(None, "grp", None, "tile"), P(None, "tile"), P(None, "tile"), P()),
        out_specs=(P(None, "grp", None, "tile"), P(None, "grp", None, "tile")),
        check_vma=False,
    )
```

```python
import functools

import jax
import jax.numpy as jnp
from jax import lax
from jax.experimental import pallas as pl
from jax.experimental.pallas import tpu as pltpu
from jax.sharding import PartitionSpec as P

HALO = 128
LANES = 128
MESH = pl.DeviceIdType.MESH
F32 = jnp.float32
BF16 = jnp.bfloat16


def split(value):
    high = value.astype(BF16)
    return high, (value - high.astype(F32)).astype(BF16)


def inverse_factor(gram):
    n, p = gram.shape[0], 8
    w = 2 * n
    rows = lax.broadcasted_iota(jnp.int32, (n, n), 0)
    cols = lax.broadcasted_iota(jnp.int32, (n, n), 1)
    both = jnp.concatenate([gram, jnp.where(rows == cols, 1.0, 0.0).astype(F32)], axis=1)
    blocks = [both[p * b:p * b + p] for b in range(n // p)]
    sub = lax.broadcasted_iota(jnp.int32, (p, w), 0)

    def full(value):
        return jnp.broadcast_to(value, (p, w))

    out = []
    for b in range(n // p):
        c = p * b
        row = [full(blocks[b][r:r + 1]) for r in range(p)]
        a = {(r, s): full(row[r][:, c + s:c + s + 1]) for r in range(p) for s in range(r, p)}
        inv = []
        for r in range(p):
            inv.append(1.0 / a[r, r])
            for s in range(r + 1, p):
                m = a[r, s] * inv[r]
                row[s] = row[s] - m * row[r]
                for t in range(s, p):
                    a[s, t] = a[s, t] - m * a[r, t]
        for bb in range(b + 1, n // p):
            col = [full(blocks[bb][:, c + s:c + s + 1]) for s in range(p)]
            for r in range(p):
                factor = col[r] * inv[r]
                for s in range(r + 1, p):
                    col[s] = col[s] - factor * a[r, s]
                blocks[bb] = blocks[bb] - factor * row[r]
        done, pivot = row[0], a[0, 0]
        for r in range(1, p):
            done = jnp.where(sub == r, row[r], done)
            pivot = jnp.where(sub == r, a[r, r], pivot)
        out.append(done * lax.rsqrt(pivot))
    return jnp.concatenate(out, axis=0)[:, n:]


def reduce_kernel(dims, x_hbm, nbr_hbm, w_hbm, coupling_hbm, res_ref, other_ref, inv_ref, coupling_ref,
                  x_ref, nbr_ref, w_ref, pairs, edge, halo, stencil, resbf, gsend, grecv, tsend, trecv,
                  hs, hr, s1, r1, s2, r2, s3, r3, loads):
    tiles, grps, low, snaps, fields, chunks = dims
    n1, n2 = low * grps, tiles // low
    me_t, me_g = lax.axis_index("tile"), lax.axis_index("grp")
    right, left = lax.rem(me_t + 1, tiles), lax.rem(me_t + tiles - 1, tiles)
    base, me_low = (me_t // low) * low, lax.rem(me_t, low)
    me1, me2 = me_low * grps + me_g, me_t // low

    def near(d):
        to = lax.rem(me1 + d, n1)
        return (base + to // grps, lax.rem(to, grps))

    def far(d):
        return (lax.rem(me2 + d, n2) * low + me_low, me_g)

    barrier = pltpu.get_barrier_semaphore()
    partners = [(left, me_g), (right, me_g)] + [near(d) for d in range(1, n1)] + [far(d) for d in range(1, n2)]
    for partner in partners:
        pl.semaphore_signal(barrier, inc=1, device_id=partner, device_id_type=MESH)

    ins = [pltpu.make_async_copy(src, dst, loads.at[i]) for i, (src, dst) in enumerate(
        ((x_hbm, x_ref), (nbr_hbm, nbr_ref), (w_hbm, w_ref), (coupling_hbm, pairs)))]
    for copy in (ins[1], ins[2], ins[0], ins[3]):
        copy.start()
    step = fields * chunks

    def chunk(q):
        return jnp.concatenate(
            [x_ref[pl.ds(f * chunks + q, snaps, stride=step), :] for f in range(fields)], axis=0)

    ins[0].wait()
    edge[0] = chunk(chunks - 1).astype(BF16)
    edge[1] = chunk(0).astype(BF16)
    pl.semaphore_wait(barrier, len(partners))
    sends = []
    for side, to in ((0, right), (1, left)):
        copy = pltpu.make_async_remote_copy(
            src_ref=edge.at[side], dst_ref=halo.at[side], send_sem=hs.at[side], recv_sem=hr.at[side],
            device_id=(to, me_g), device_id_type=MESH)
        copy.start()
        sends.append(copy)

    ins[1].wait()
    ins[2].wait()
    iota = lax.broadcasted_iota(jnp.int32, (3 * LANES, LANES), 0)
    for q in range(chunks):
        here = slice(q * LANES, (q + 1) * LANES)
        total = jnp.zeros((3 * LANES, LANES), F32)
        for j in range(nbr_ref.shape[0]):
            total = total + jnp.where(iota == nbr_ref[j:j + 1, here] - q * LANES, w_ref[j:j + 1, here], 0.0)
        stencil[q] = total.astype(BF16)

    own = [chunk(q).astype(BF16) for q in range(chunks)]

    def part(q, d, block):
        return jnp.dot(block, stencil[q, d * LANES:(d + 1) * LANES, :], preferred_element_type=F32)

    rows = snaps * fields
    highs, lows = [None] * chunks, [None] * chunks
    res_copies = []
    early = 1

    def send_res(q):
        for d in range(1, grps):
            at = pl.ds(q * rows, rows)
            copy = pltpu.make_async_remote_copy(
                src_ref=resbf.at[at], dst_ref=other_ref.at[d - 1, at],
                send_sem=s3.at[d - 1, q], recv_sem=r3.at[d - 1, q],
                device_id=(me_t, lax.rem(me_g + d, grps)), device_id_type=MESH)
            copy.start()
            res_copies.append(copy)

    def finish(q, stencil_sum):
        res = chunk(q) - stencil_sum
        res_ref[q * rows:(q + 1) * rows, :] = res
        highs[q], lows[q] = split(res)
        resbf[q * rows:(q + 1) * rows, :] = highs[q]

    sums = []
    for q in range(chunks):
        total = None
        for d in range(3):
            if 0 <= q + d - 1 < chunks:
                term = part(q, d, own[q + d - 1])
                total = term if total is None else total + term
        sums.append(total)
    for q in range(1, chunks - 1):
        finish(q, sums[q])
        if q == early:
            send_res(q)
    for copy in sends:
        copy.wait()
    finish(0, sums[0] + part(0, 0, halo[0]))
    finish(chunks - 1, sums[-1] + part(chunks - 1, 2, halo[1]))

    gram = jnp.zeros((2 * snaps, snaps), F32)
    for f in range(fields):
        at = slice(f * snaps, (f + 1) * snaps)
        high = jnp.concatenate([h[at] for h in highs], axis=1)
        low_part = jnp.concatenate([h[at] for h in lows], axis=1)
        gram = gram + lax.dot_general(jnp.concatenate([high, low_part], axis=0), high,
                                      (((1,), (1,)), ((), ())), preferred_element_type=F32)
    gram = gram[:snaps] + (gram[snaps:] + gram[snaps:].T)
    gram = gram * (1.0 / (fields * chunks * LANES * tiles * grps))
    half = snaps // 2
    gsend[...] = jnp.concatenate([gram[:half], gram[half:]], axis=1)

    def exchange(count, where, src, dst, ss, rs):
        copies = []
        for d in range(1, count):
            copy = pltpu.make_async_remote_copy(
                src_ref=src, dst_ref=dst.at[d - 1], send_sem=ss.at[d - 1], recv_sem=rs.at[d - 1],
                device_id=where(d), device_id_type=MESH)
            copy.start()
            copies.append(copy)
        return copies

    total = gsend[...]
    copies = exchange(n1, near, gsend, grecv, s1, r1)
    for q in range(chunks):
        if q != early:
            send_res(q)
    for d, copy in enumerate(copies):
        copy.wait_recv()
        total = total + grecv[d]
    tsend[...] = total
    far_copies = exchange(n2, far, tsend, trecv, s2, r2)
    for d, copy in enumerate(far_copies):
        copy.wait_recv()
        total = total + trecv[d]
    gram = jnp.concatenate([total[:, :snaps], total[:, snaps:]], axis=0)
    inv_ref[...] = inverse_factor(gram)
    ins[3].wait()
    coupling_ref[...] = pairs[...]
    for copy in copies + far_copies:
        copy.wait_send()
    for copy in res_copies:
        copy.wait()


def basis_kernel(dims, inv_ref, res_ref, other_ref, coupling_ref, basis_hbm, coupled_hbm, basis_ref, coupled_ref, sems):
    tiles, grps, low, snaps, fields, chunks = dims
    me_g = lax.axis_index("grp")
    rows, step = snaps * fields, fields * chunks
    high, low_part = split(inv_ref[...])
    three = jnp.concatenate([high, low_part, high], axis=1)
    two = jnp.concatenate([high, low_part], axis=1)
    rows_at = lax.broadcasted_iota(jnp.int32, (grps, grps), 0)
    cols_at = lax.broadcasted_iota(jnp.int32, (grps, grps), 1)

    def scale(d):
        here = (rows_at == me_g) & (cols_at == lax.rem(me_g + grps - d, grps))
        kept = jnp.where(here, coupling_ref[...], 0.0)
        return jnp.sum(jnp.sum(kept, axis=1, keepdims=True), axis=0, keepdims=True)

    own_scale = scale(0)
    scales = [scale(d) for d in range(1, grps)]
    places = [(pl.ds(q * rows + f * snaps, snaps), pl.ds(f * chunks + q, snaps, stride=step))
              for f in range(fields) for q in range(chunks)]
    for at, to in places:
        rh, rl = split(res_ref[at, :])
        basis = jnp.dot(three, jnp.concatenate([rh, rh, rl], axis=0), preferred_element_type=F32)
        basis_ref[to, :] = basis
    first = pltpu.make_async_copy(basis_ref, basis_hbm, sems.at[0])
    first.start()
    for at, to in places:
        rounded = basis_ref[to, :].astype(BF16).astype(F32)
        mixed = own_scale * rounded
        for d in range(1, grps):
            there = other_ref[d - 1, at, :]
            theirs = jnp.dot(two, jnp.concatenate([there, there], axis=0), preferred_element_type=F32)
            mixed = mixed + scales[d - 1] * theirs.astype(BF16).astype(F32)
        coupled_ref[to, :] = rounded + mixed
    second = pltpu.make_async_copy(coupled_ref, coupled_hbm, sems.at[1])
    second.start()
    first.wait()
    second.wait()


def local(mesh, snapshots, neighbors, weights, coupling):
    tiles, grps = mesh.shape["tile"], mesh.shape["grp"]
    snaps, _, fields, cells = snapshots.shape
    chunks = cells // LANES
    low = 4
    dims = (tiles, grps, low, snaps, fields, chunks)
    n1, n2 = low * grps, tiles // low
    rows = snaps * fields
    count = rows * chunks
    x = snapshots.reshape(count, LANES)
    vmem = pl.BlockSpec(memory_space=pltpu.VMEM)
    dma = lambda n: pltpu.SemaphoreType.DMA((n,))
    res, other, inverse, pairs = pl.pallas_call(
        functools.partial(reduce_kernel, dims),
        out_shape=(jax.ShapeDtypeStruct((count, LANES), F32),
                   jax.ShapeDtypeStruct((grps - 1, count, LANES), BF16),
                   jax.ShapeDtypeStruct((snaps, snaps), F32),
                   jax.ShapeDtypeStruct(coupling.shape, F32)),
        in_specs=[pl.BlockSpec(memory_space=pltpu.HBM)] * 4,
        out_specs=(vmem,) * 4,
        scratch_shapes=[
            pltpu.VMEM((count, LANES), F32),
            pltpu.VMEM(neighbors.shape, jnp.int32),
            pltpu.VMEM(weights.shape, F32),
            pltpu.VMEM(coupling.shape, F32),
            pltpu.VMEM((2, rows, LANES), BF16),
            pltpu.VMEM((2, rows, LANES), BF16),
            pltpu.VMEM((chunks, 3 * LANES, LANES), BF16),
            pltpu.VMEM((count, LANES), BF16),
            pltpu.VMEM((snaps // 2, 2 * snaps), F32),
            pltpu.VMEM((n1 - 1, snaps // 2, 2 * snaps), F32),
            pltpu.VMEM((snaps // 2, 2 * snaps), F32),
            pltpu.VMEM((n2 - 1, snaps // 2, 2 * snaps), F32),
            dma(2), dma(2), dma(n1 - 1), dma(n1 - 1), dma(n2 - 1), dma(n2 - 1), pltpu.SemaphoreType.DMA((grps - 1, chunks)), pltpu.SemaphoreType.DMA((grps - 1, chunks)),
            dma(4),
        ],
        compiler_params=pltpu.CompilerParams(
            collective_id=0, has_side_effects=True, vmem_limit_bytes=32 * 2 ** 20),
        name="reduce",
    )(*[pltpu.with_memory_space_constraint(a, pltpu.HBM) for a in (x, neighbors, weights, coupling)])
    basis, coupled = pl.pallas_call(
        functools.partial(basis_kernel, dims),
        out_shape=(jax.ShapeDtypeStruct((count, LANES), F32),) * 2,
        in_specs=[vmem] * 4,
        out_specs=(pl.BlockSpec(memory_space=pltpu.HBM),) * 2,
        scratch_shapes=[pltpu.VMEM((count, LANES), F32), pltpu.VMEM((count, LANES), F32), dma(2)],
        compiler_params=pltpu.CompilerParams(vmem_limit_bytes=32 * 2 ** 20),
        name="basis",
    )(inverse, res, other, pairs)
    return basis.reshape(snapshots.shape), coupled.reshape(snapshots.shape)


def solution(mesh):
    return jax.shard_map(
        functools.partial(local, mesh),
        mesh=mesh,
        in_specs=(P(None, "grp", None, "tile"), P(None, "tile"), P(None, "tile"), P()),
        out_specs=(P(None, "grp", None, "tile"), P(None, "grp", None, "tile")),
        check_vma=False,
    )
```

```python
import functools

import jax
import jax.numpy as jnp
from jax import lax
from jax.experimental import pallas as pl
from jax.experimental.pallas import tpu as pltpu
from jax.sharding import PartitionSpec as P

HALO = 128
LANES = 128
MESH = pl.DeviceIdType.MESH
F32 = jnp.float32
BF16 = jnp.bfloat16


def split(value):
    high = value.astype(BF16)
    return high, (value - high.astype(F32)).astype(BF16)


def inverse_factor(gram):
    n, p = gram.shape[0], 8
    w = 2 * n
    rows = lax.broadcasted_iota(jnp.int32, (n, n), 0)
    cols = lax.broadcasted_iota(jnp.int32, (n, n), 1)
    both = jnp.concatenate([gram, jnp.where(rows == cols, 1.0, 0.0).astype(F32)], axis=1)
    blocks = [both[p * b:p * b + p] for b in range(n // p)]
    sub = lax.broadcasted_iota(jnp.int32, (p, w), 0)

    def full(value):
        return jnp.broadcast_to(value, (p, w))

    out = []
    for b in range(n // p):
        c = p * b
        row = [full(blocks[b][r:r + 1]) for r in range(p)]
        a = {(r, s): full(row[r][:, c + s:c + s + 1]) for r in range(p) for s in range(r, p)}
        inv = []
        for r in range(p):
            inv.append(1.0 / a[r, r])
            for s in range(r + 1, p):
                m = a[r, s] * inv[r]
                row[s] = row[s] - m * row[r]
                for t in range(s, p):
                    a[s, t] = a[s, t] - m * a[r, t]
        for bb in range(b + 1, n // p):
            col = [full(blocks[bb][:, c + s:c + s + 1]) for s in range(p)]
            for r in range(p):
                factor = col[r] * inv[r]
                for s in range(r + 1, p):
                    col[s] = col[s] - factor * a[r, s]
                blocks[bb] = blocks[bb] - factor * row[r]
        done, pivot = row[0], a[0, 0]
        for r in range(1, p):
            done = jnp.where(sub == r, row[r], done)
            pivot = jnp.where(sub == r, a[r, r], pivot)
        out.append(done * lax.rsqrt(pivot))
    return jnp.concatenate(out, axis=0)[:, n:]


def reduce_kernel(dims, x_hbm, nbr_hbm, w_hbm, coupling_hbm, res_ref, other_ref, inv_ref, coupling_ref,
                  x_ref, nbr_ref, w_ref, pairs, edge, halo, stencil, resbf, gsend, grecv, tsend, trecv,
                  hs, hr, s1, r1, s2, r2, s3, r3, loads):
    tiles, grps, low, snaps, fields, chunks = dims
    n1, n2 = low * grps, tiles // low
    me_t, me_g = lax.axis_index("tile"), lax.axis_index("grp")
    right, left = lax.rem(me_t + 1, tiles), lax.rem(me_t + tiles - 1, tiles)
    base, me_low = (me_t // low) * low, lax.rem(me_t, low)
    me1, me2 = me_low * grps + me_g, me_t // low

    def near(d):
        to = lax.rem(me1 + d, n1)
        return (base + to // grps, lax.rem(to, grps))

    def far(d):
        return (lax.rem(me2 + d, n2) * low + me_low, me_g)

    barrier = pltpu.get_barrier_semaphore()
    partners = [(left, me_g), (right, me_g)] + [near(d) for d in range(1, n1)] + [far(d) for d in range(1, n2)]
    for partner in partners:
        pl.semaphore_signal(barrier, inc=1, device_id=partner, device_id_type=MESH)

    ins = [pltpu.make_async_copy(src, dst, loads.at[i]) for i, (src, dst) in enumerate(
        ((x_hbm, x_ref), (nbr_hbm, nbr_ref), (w_hbm, w_ref), (coupling_hbm, pairs)))]
    for copy in (ins[1], ins[2], ins[0], ins[3]):
        copy.start()
    step = fields * chunks

    def chunk(q):
        return jnp.concatenate(
            [x_ref[pl.ds(f * chunks + q, snaps, stride=step), :] for f in range(fields)], axis=0)

    ins[0].wait()
    edge[0] = chunk(chunks - 1).astype(BF16)
    edge[1] = chunk(0).astype(BF16)
    pl.semaphore_wait(barrier, len(partners))
    sends = []
    for side, to in ((0, right), (1, left)):
        copy = pltpu.make_async_remote_copy(
            src_ref=edge.at[side], dst_ref=halo.at[side], send_sem=hs.at[side], recv_sem=hr.at[side],
            device_id=(to, me_g), device_id_type=MESH)
        copy.start()
        sends.append(copy)

    ins[1].wait()
    ins[2].wait()
    iota = lax.broadcasted_iota(jnp.int32, (3 * LANES, LANES), 0)
    for q in range(chunks):
        here = slice(q * LANES, (q + 1) * LANES)
        total = jnp.zeros((3 * LANES, LANES), F32)
        for j in range(nbr_ref.shape[0]):
            total = total + jnp.where(iota == nbr_ref[j:j + 1, here] - q * LANES, w_ref[j:j + 1, here], 0.0)
        stencil[q] = total.astype(BF16)

    own = [chunk(q).astype(BF16) for q in range(chunks)]

    def part(q, d, block):
        return jnp.dot(block, stencil[q, d * LANES:(d + 1) * LANES, :], preferred_element_type=F32)

    rows = snaps * fields
    highs, lows = [None] * chunks, [None] * chunks
    res_copies = []
    early = 1

    def send_res(q):
        for d in range(1, grps):
            at = pl.ds(q * rows, rows)
            copy = pltpu.make_async_remote_copy(
                src_ref=resbf.at[at], dst_ref=other_ref.at[d - 1, at],
                send_sem=s3.at[d - 1, q], recv_sem=r3.at[d - 1, q],
                device_id=(me_t, lax.rem(me_g + d, grps)), device_id_type=MESH)
            copy.start()
            res_copies.append(copy)

    def finish(q, stencil_sum):
        res = chunk(q) - stencil_sum
        res_ref[q * rows:(q + 1) * rows, :] = res
        highs[q], lows[q] = split(res)
        resbf[q * rows:(q + 1) * rows, :] = highs[q]

    sums = []
    for q in range(chunks):
        total = None
        for d in range(3):
            if 0 <= q + d - 1 < chunks:
                term = part(q, d, own[q + d - 1])
                total = term if total is None else total + term
        sums.append(total)
    for q in range(1, chunks - 1):
        finish(q, sums[q])
        if q == early:
            send_res(q)

    def products(which):
        total = jnp.zeros((2 * snaps, snaps), F32)
        for f in range(fields):
            at = slice(f * snaps, (f + 1) * snaps)
            high = jnp.concatenate([highs[q][at] for q in which], axis=1)
            low_part = jnp.concatenate([lows[q][at] for q in which], axis=1)
            total = total + lax.dot_general(jnp.concatenate([high, low_part], axis=0), high,
                                            (((1,), (1,)), ((), ())), preferred_element_type=F32)
        return total

    inner = products(list(range(1, chunks - 1)))
    for copy in sends:
        copy.wait()
    finish(0, sums[0] + part(0, 0, halo[0]))
    finish(chunks - 1, sums[-1] + part(chunks - 1, 2, halo[1]))

    gram = inner + products([0, chunks - 1])
    gram = gram[:snaps] + (gram[snaps:] + gram[snaps:].T)
    gram = gram * (1.0 / (fields * chunks * LANES * tiles * grps))
    half = snaps // 2
    gsend[...] = jnp.concatenate([gram[:half], gram[half:]], axis=1)

    def exchange(count, where, src, dst, ss, rs):
        copies = []
        for d in range(1, count):
            copy = pltpu.make_async_remote_copy(
                src_ref=src, dst_ref=dst.at[d - 1], send_sem=ss.at[d - 1], recv_sem=rs.at[d - 1],
                device_id=where(d), device_id_type=MESH)
            copy.start()
            copies.append(copy)
        return copies

    total = gsend[...]
    copies = exchange(n1, near, gsend, grecv, s1, r1)
    for q in range(chunks):
        if q != early:
            send_res(q)
    for d, copy in enumerate(copies):
        copy.wait_recv()
        total = total + grecv[d]
    tsend[...] = total
    far_copies = exchange(n2, far, tsend, trecv, s2, r2)
    for d, copy in enumerate(far_copies):
        copy.wait_recv()
        total = total + trecv[d]
    gram = jnp.concatenate([total[:, :snaps], total[:, snaps:]], axis=0)
    inv_ref[...] = inverse_factor(gram)
    ins[3].wait()
    coupling_ref[...] = pairs[...]
    for copy in copies + far_copies:
        copy.wait_send()
    for copy in res_copies:
        copy.wait()


def basis_kernel(dims, inv_ref, res_ref, other_ref, coupling_ref, basis_hbm, coupled_hbm, basis_ref, coupled_ref, sems):
    tiles, grps, low, snaps, fields, chunks = dims
    me_g = lax.axis_index("grp")
    rows, step = snaps * fields, fields * chunks
    high, low_part = split(inv_ref[...])
    three = jnp.concatenate([high, low_part, high], axis=1)
    two = jnp.concatenate([high, low_part], axis=1)
    rows_at = lax.broadcasted_iota(jnp.int32, (grps, grps), 0)
    cols_at = lax.broadcasted_iota(jnp.int32, (grps, grps), 1)

    def scale(d):
        here = (rows_at == me_g) & (cols_at == lax.rem(me_g + grps - d, grps))
        kept = jnp.where(here, coupling_ref[...], 0.0)
        return jnp.sum(jnp.sum(kept, axis=1, keepdims=True), axis=0, keepdims=True)

    own_scale = scale(0)
    scales = [scale(d) for d in range(1, grps)]
    places = [(pl.ds(q * rows + f * snaps, snaps), pl.ds(f * chunks + q, snaps, stride=step))
              for f in range(fields) for q in range(chunks)]
    for at, to in places:
        rh, rl = split(res_ref[at, :])
        basis = jnp.dot(three, jnp.concatenate([rh, rh, rl], axis=0), preferred_element_type=F32)
        basis_ref[to, :] = basis
    first = pltpu.make_async_copy(basis_ref, basis_hbm, sems.at[0])
    first.start()
    for at, to in places:
        rounded = basis_ref[to, :].astype(BF16).astype(F32)
        mixed = own_scale * rounded
        for d in range(1, grps):
            there = other_ref[d - 1, at, :]
            theirs = jnp.dot(two, jnp.concatenate([there, there], axis=0), preferred_element_type=F32)
            mixed = mixed + scales[d - 1] * theirs.astype(BF16).astype(F32)
        coupled_ref[to, :] = rounded + mixed
    second = pltpu.make_async_copy(coupled_ref, coupled_hbm, sems.at[1])
    second.start()
    first.wait()
    second.wait()


def local(mesh, snapshots, neighbors, weights, coupling):
    tiles, grps = mesh.shape["tile"], mesh.shape["grp"]
    snaps, _, fields, cells = snapshots.shape
    chunks = cells // LANES
    low = 4
    dims = (tiles, grps, low, snaps, fields, chunks)
    n1, n2 = low * grps, tiles // low
    rows = snaps * fields
    count = rows * chunks
    x = snapshots.reshape(count, LANES)
    vmem = pl.BlockSpec(memory_space=pltpu.VMEM)
    dma = lambda n: pltpu.SemaphoreType.DMA((n,))
    res, other, inverse, pairs = pl.pallas_call(
        functools.partial(reduce_kernel, dims),
        out_shape=(jax.ShapeDtypeStruct((count, LANES), F32),
                   jax.ShapeDtypeStruct((grps - 1, count, LANES), BF16),
                   jax.ShapeDtypeStruct((snaps, snaps), F32),
                   jax.ShapeDtypeStruct(coupling.shape, F32)),
        in_specs=[pl.BlockSpec(memory_space=pltpu.HBM)] * 4,
        out_specs=(vmem,) * 4,
        scratch_shapes=[
            pltpu.VMEM((count, LANES), F32),
            pltpu.VMEM(neighbors.shape, jnp.int32),
            pltpu.VMEM(weights.shape, F32),
            pltpu.VMEM(coupling.shape, F32),
            pltpu.VMEM((2, rows, LANES), BF16),
            pltpu.VMEM((2, rows, LANES), BF16),
            pltpu.VMEM((chunks, 3 * LANES, LANES), BF16),
            pltpu.VMEM((count, LANES), BF16),
            pltpu.VMEM((snaps // 2, 2 * snaps), F32),
            pltpu.VMEM((n1 - 1, snaps // 2, 2 * snaps), F32),
            pltpu.VMEM((snaps // 2, 2 * snaps), F32),
            pltpu.VMEM((n2 - 1, snaps // 2, 2 * snaps), F32),
            dma(2), dma(2), dma(n1 - 1), dma(n1 - 1), dma(n2 - 1), dma(n2 - 1), pltpu.SemaphoreType.DMA((grps - 1, chunks)), pltpu.SemaphoreType.DMA((grps - 1, chunks)),
            dma(4),
        ],
        compiler_params=pltpu.CompilerParams(
            collective_id=0, has_side_effects=True, vmem_limit_bytes=32 * 2 ** 20),
        name="reduce",
    )(*[pltpu.with_memory_space_constraint(a, pltpu.HBM) for a in (x, neighbors, weights, coupling)])
    basis, coupled = pl.pallas_call(
        functools.partial(basis_kernel, dims),
        out_shape=(jax.ShapeDtypeStruct((count, LANES), F32),) * 2,
        in_specs=[vmem] * 4,
        out_specs=(pl.BlockSpec(memory_space=pltpu.HBM),) * 2,
        scratch_shapes=[pltpu.VMEM((count, LANES), F32), pltpu.VMEM((count, LANES), F32), dma(2)],
        compiler_params=pltpu.CompilerParams(vmem_limit_bytes=32 * 2 ** 20),
        name="basis",
    )(inverse, res, other, pairs)
    return basis.reshape(snapshots.shape), coupled.reshape(snapshots.shape)


def solution(mesh):
    return jax.shard_map(
        functools.partial(local, mesh),
        mesh=mesh,
        in_specs=(P(None, "grp", None, "tile"), P(None, "tile"), P(None, "tile"), P()),
        out_specs=(P(None, "grp", None, "tile"), P(None, "grp", None, "tile")),
        check_vma=False,
    )
```
